128 devices in a mesh: owner: 32 (over y, z, core), task: 4 (over x).
Axes of the slice: x: 4, y: 4, z: 4, core: 2. Of those that a mesh axis runs over, the one named last changes fastest.
Arguments:
- amplitudes: bfloat16 [768, 20, 32, 256], P('owner'), may hold values from -6 to 6
- integrals: bfloat16 [20, 32, 8192, 256], P(None, 'owner', 'task'), may hold values from -0.015625 to 0.015625
- nonzero_tiles: int32 [32, 18], replicated, may hold values from 0 to 19, as said below
Outputs:
- ladder: float32 [768, 8192], P('owner', 'task')
The draws below stay inside these ranges and needn't reach their ends.
Inputs may be any that keep to these rules, and one draw needn't show every extreme that they name: `nonzero_tiles`: each row o holds 18 different tile slots of owner o; tiles not listed do not enter.
All inputs are finite; a program needn't handle non-finite values.
Results may differ from the reference program's by a relative error of at most 0.0003.
Values may be sent and summed in bfloat16 or wider, within the bound.
No kernel may reach another device: no remote copies, remote signals or barrier semaphores. Data moves between devices by JAX's collectives and lax.ppermute only.
A program may use at most 128 MiB of HBM per device.

```python
import jax
import jax.numpy as jnp
from jax import lax

CT = 256
TILES_DEV = 20
LIVE = 18
PAIRS = 768
AB = 8192
N_OWNER = 32


def draw_nonzero_tiles(key, part):
    key = jax.random.fold_in(key, 5)
    keys = jax.random.split(key, N_OWNER + 1)
    rows = jax.vmap(lambda single: jax.random.permutation(single, TILES_DEV)[:LIVE])(keys[:N_OWNER])
    middle = jax.random.permutation(keys[N_OWNER], TILES_DEV - 2) + 1
    ends = jnp.array([TILES_DEV - 1, 0], dtype=jnp.int32)
    first = jnp.concatenate([ends, middle.astype(jnp.int32)])[:LIVE]
    rows = rows.astype(jnp.int32).at[0].set(first)
    return rows.astype(jnp.int32)


def steps_of(rng, dims, cuts, smallest, largest):
    loudness, own = 1.0, jax.random.fold_in(rng, 6)
    for position, parts in cuts:
        steps = jnp.exp(jax.random.uniform(jax.random.fold_in(own, position), (parts,), jnp.float32, smallest / len(cuts), largest / len(cuts)))
        loudness = loudness * jnp.repeat(steps, dims[position] // parts).reshape([-1 if axis == position else 1 for axis in range(len(dims))])
    return loudness


def scatter_about(own_key, shape, deviation, most, shards=(), held_as=jnp.bfloat16):
    drawn = jax.random.normal(own_key, shape, jnp.float32) * deviation
    if len(shards) > 0:
        drawn = steps_of(own_key, shape, shards, -0.22, 0.18) * drawn
    return jnp.clip(drawn, min=-most, max=most).astype(held_as)


def setup_inputs(seed: int = 0) -> dict:
    key_list = jax.random.split(jax.random.key(seed), 4)
    amplitudes = scatter_about(key_list[0], (PAIRS, TILES_DEV, N_OWNER, CT), 1.0, 6.0, ((0, 32),))
    integrals = scatter_about(key_list[1], (TILES_DEV, N_OWNER, AB, CT), (LIVE * CT * N_OWNER) ** -0.5, 0.015625, ((1, 32), (2, 4)))
    nonzero_tiles = draw_nonzero_tiles(jax.random.fold_in(key_list[3], 71), 0)
    return dict(amplitudes=amplitudes, integrals=integrals, nonzero_tiles=nonzero_tiles)


def reference(amplitudes, integrals, nonzero_tiles):
    def one_owner(total, owner):
        rows = lax.dynamic_index_in_dim(nonzero_tiles, owner, 0, False)
        amp_owner = lax.dynamic_index_in_dim(amplitudes, owner, 2, False)
        amp_live = jnp.take(amp_owner, rows, axis=1).astype(jnp.float32)
        int_owner = lax.dynamic_index_in_dim(integrals, owner, 1, False)
        int_live = jnp.take(int_owner, rows, axis=0).astype(jnp.float32)
        return total + jnp.einsum("plx,lax->pa", amp_live, int_live), None

    start = jnp.zeros((amplitudes.shape[0], integrals.shape[2]), jnp.float32)
    owners = jnp.arange(N_OWNER, dtype=jnp.int32)
    ladder, unused = lax.scan(one_owner, start, owners)
    return ladder
```

```python
import functools

import jax
import jax.numpy as jnp
from jax import lax
from jax.experimental import pallas as pl
from jax.experimental.pallas import tpu as pltpu
from jax.sharding import PartitionSpec as P

OWNERS, TASKS, SIDE = 32, 4, 4
QUARTER = 2
SHARED = QUARTER * TASKS
BUNDLE = 5
GROUP = 8
F32 = jnp.float32


def owner_at(y, z, c):
    return ((y % SIDE) * SIDE + z % SIDE) * 2 + c


def owner_perm(move):
    return [
        (owner_at(y, z, c), owner_at(*move(y, z, c)))
        for y in range(SIDE)
        for z in range(SIDE)
        for c in range(2)
    ]


def along(step, cores_swapped):
    return owner_perm(
        lambda y, z, c: (y, z + step, c) if c == cores_swapped else (y + step, z, c)
    )


def shift_task(step):
    return [(t, (t + step) % TASKS) for t in range(TASKS)]


def pack_kernel(by_task, first, nz_ref, amp_ref, out_ref, listed, source, nz_sem, sem):
    owners, count, pairs, ct = out_ref.shape
    tiles = source.shape[0]
    start = first + (lax.axis_index("task") * count if by_task else 0)
    copies = [pltpu.make_async_copy(nz_ref, listed, nz_sem)]
    for k in range(tiles):
        copies.append(pltpu.make_async_copy(amp_ref.at[:, k], source.at[k], sem.at[k]))
    for copy in copies:
        copy.start()

    n = pairs * GROUP
    row = lax.broadcasted_iota(jnp.int32, (n, n), 0)
    column = lax.broadcasted_iota(jnp.int32, (n, n), 1)
    turn = (row == column % GROUP * pairs + column // GROUP).astype(F32).astype(source.dtype)
    for copy in copies:
        copy.wait()

    def give(i, carry):
        for o in range(owners):
            j = o % GROUP
            rows = source[listed[start + i, o], :, o - j : o - j + GROUP].reshape(n, ct)
            block = jnp.dot(turn[j * pairs : (j + 1) * pairs], rows, preferred_element_type=F32)
            out_ref[o, i] = block.astype(out_ref.dtype)
        return carry

    lax.fori_loop(0, count, give, 0)


def pack(amplitudes, listed, first, count, by_task):
    pairs, tiles, owners, ct = amplitudes.shape
    anywhere = pl.BlockSpec(memory_space=pltpu.HBM)
    return pl.pallas_call(
        functools.partial(pack_kernel, by_task, first),
        in_specs=[anywhere, anywhere],
        out_specs=pl.BlockSpec(memory_space=pltpu.VMEM),
        out_shape=jax.ShapeDtypeStruct((owners, count, pairs, ct), amplitudes.dtype),
        scratch_shapes=[
            pltpu.SMEM(listed.shape, jnp.int32),
            pltpu.VMEM((tiles, pairs, owners, ct), amplitudes.dtype),
            pltpu.SemaphoreType.DMA,
            pltpu.SemaphoreType.DMA((tiles,)),
        ],
        compiler_params=pltpu.CompilerParams(vmem_limit_bytes=60 << 20),
        cost_estimate=pl.CostEstimate(
            flops=2 * count * owners * pairs * pairs * GROUP * ct * 8,
            bytes_accessed=2 * tiles * owners * pairs * ct,
            transcendentals=0,
        ),
        name="pack_shared" if by_task else "pack_direct",
    )(listed, amplitudes)


def product_kernel(counts, sides, on_top, inside, slots_ref, core_ref, places_ref, *refs):
    refs = list(refs)

    def take(n):
        taken = refs[:n]
        del refs[:n]
        return taken

    piece_refs, (int_ref,) = take(len(counts)), take(1)
    start_refs, out_refs = take(sides * on_top), take(sides)
    parts = out_refs if inside else take(sides)
    held, rhs, held_sem, rhs_sem, part_sem, out_sem = refs
    blocks, steps, pairs, tile = parts[0].shape
    where = [(piece, j) for piece, n in zip(piece_refs, counts, strict=True) for j in range(n)]
    slots = len(where)

    def columns(n):
        return pl.ds(n * tile if isinstance(n, int) else pl.multiple_of(n * tile, tile), tile)

    def fetch(n, l):
        return pltpu.make_async_copy(
            int_ref.at[slots_ref[l], 0, columns(n)], rhs.at[l, columns(n)], rhs_sem.at[n, l]
        )

    def fetch_rows(i, l):
        piece, j = where[l]
        return pltpu.make_async_copy(
            piece.at[:, core_ref[i], j], held.at[i, l], held_sem.at[i, l]
        )

    def fetch_start(n, i):
        return pltpu.make_async_copy(
            start_refs[i].at[:, n], parts[i].at[:, n], part_sem.at[n, i]
        )

    def put(n, i):
        return pltpu.make_async_copy(
            parts[i].at[:, n], out_refs[i].at[:, n], out_sem.at[n, i]
        )

    def bring(n, group):
        for l in group:
            fetch(n, l).start()
        if on_top and group[0] == 0:
            for i in range(sides):
                fetch_start(n, i).start()

    groups = [range(l, min(l + BUNDLE, slots)) for l in range(0, slots, BUNDLE)]

    def step(n, first):
        here = columns(n)
        total = [None] * sides
        for group in groups:
            for l in group:
                if first:
                    fetch_rows(0, l).wait()
                fetch(n, l).wait()

            @pl.when(n + 1 < steps)
            def _(group=group):
                bring(n + 1, group)

            for i in range(sides):
                for l in group:
                    if first and i > 0:
                        fetch_rows(i, l).wait()
                for l in group:
                    term = lax.dot_general(
                        held[i, l].reshape(blocks * pairs, -1),
                        rhs[l, here],
                        (((1,), (1,)), ((), ())),
                        preferred_element_type=F32,
                    )
                    total[i] = term if total[i] is None else total[i] + term
        for i in range(sides):
            sums = total[i].reshape(blocks, pairs, tile)
            if on_top:
                fetch_start(n, i).wait()
            for b in range(blocks):
                place = places_ref[i * blocks + b]
                parts[i][place, n] = sums[b] + parts[i][place, n] if on_top else sums[b]
            if not inside:
                put(n, i).start()

    for group in groups:
        for i in range(sides):
            for l in group:
                fetch_rows(i, l).start()
        bring(0, group)
    step(0, True)
    lax.fori_loop(1, steps, lambda n, carry: (step(n, False), carry)[1], 0)
    for n in range(0 if inside else steps):
        for i in range(sides):
            put(n, i).wait()


def product(pieces, integrals, slots, cores, places, start=(), spare=0, tile=512, name="product"):
    owners, _, pairs, ct = pieces[0].shape
    counts = [piece.shape[1] for piece in pieces]
    blocks, ab, sides, count = owners // 2, integrals.shape[2], cores.shape[0], sum(counts)
    pieces = [piece.reshape(blocks, 2, *piece.shape[1:]) for piece in pieces]
    small = pl.BlockSpec(memory_space=pltpu.SMEM)
    anywhere = pl.BlockSpec(memory_space=pl.ANY)
    whole = pl.BlockSpec(memory_space=pltpu.VMEM)
    steps, inside = ab // tile, spare > 0
    part = (blocks, steps, pairs, tile)
    return pl.pallas_call(
        functools.partial(product_kernel, counts, sides, len(start) > 0, inside),
        in_specs=[small] * 3 + [anywhere] * (len(pieces) + 1 + len(start)),
        out_specs=[whole if inside else anywhere] * sides,
        out_shape=[jax.ShapeDtypeStruct(part, F32)] * sides,
        scratch_shapes=[pltpu.VMEM(part, F32)] * (0 if inside else sides)
        + [
            pltpu.VMEM((sides, count, blocks, pairs, ct), pieces[0].dtype),
            pltpu.VMEM((count, ab, ct), integrals.dtype),
            pltpu.SemaphoreType.DMA((sides, count)),
            pltpu.SemaphoreType.DMA((steps, count)),
            pltpu.SemaphoreType.DMA((steps, sides)),
            pltpu.SemaphoreType.DMA((steps, sides)),
        ],
        compiler_params=pltpu.CompilerParams(vmem_limit_bytes=(60 << 20) - spare),
        cost_estimate=pl.CostEstimate(
            flops=2 * sides * blocks * pairs * ab * count * ct,
            bytes_accessed=ab * count * ct * 2 + sides * blocks * pairs * ab * 4,
            transcendentals=0,
        ),
        name=name,
    )(slots, cores, places, *pieces, integrals, *start)


def sum_to_first(part, swapped):
    def send(x, step):
        return lax.ppermute(x, "owner", along(step, swapped))

    return part[0] + send(part[1], 1) + send(part[3], 3) + send(part[2], 2)


def per_device(amplitudes, integrals, nonzero_tiles):
    owner = lax.axis_index("owner")
    task = lax.axis_index("task")
    y, z, c = owner // (2 * SIDE), owner // 2 % SIDE, owner % 2
    pairs = amplitudes.shape[0]
    ab = integrals.shape[2]
    mine = lax.dynamic_index_in_dim(nonzero_tiles, owner, 0, False)

    listed = nonzero_tiles.T
    live = listed.shape[0]
    shared = pack(amplitudes, listed, 0, QUARTER, True)
    quarter = lax.all_to_all(shared, "owner", 0, 0, tiled=True)
    direct = pack(amplitudes, listed, SHARED, live - SHARED, False)
    direct = lax.all_to_all(direct, "owner", 0, 0, tiled=True)
    before = lax.ppermute(quarter, "task", shift_task(1))
    after = lax.ppermute(quarter, "task", shift_task(-1))
    cut = QUARTER // 2
    across = [
        lax.ppermute(before[:, :cut], "task", shift_task(1)),
        lax.ppermute(after[:, cut:], "task", shift_task(-1)),
    ]

    def slots_of(t):
        return t % TASKS * QUARTER + jnp.arange(QUARTER)

    order = [slots_of(task), slots_of(task - 1), slots_of(task + 1), slots_of(task + 2)]
    slots = jnp.take(mine, jnp.concatenate([*order, jnp.arange(SHARED, live)]))
    near = 3 * QUARTER

    def places(core):
        dy = (jnp.repeat(jnp.arange(SIDE), SIDE) - y) % SIDE
        dz = (jnp.tile(jnp.arange(SIDE), SIDE) - z) % SIDE
        return jnp.where(core == 0, dz * SIDE + dy, dy * SIDE + dz)

    cores = jnp.stack([1 - c, c])
    where_to = jnp.concatenate([places(1 - c), places(c)])
    half = SIDE * SIDE
    both = product(
        [quarter, before, after], integrals, slots[:near], cores, where_to, name="product_near"
    )
    other, own = product(
        across, integrals, slots[near:SHARED], cores, where_to, both, name="product_across"
    )
    late = slots[SHARED:]
    (other,) = product(
        [direct], integrals, late, cores[:1], where_to[:half], [other], 6 << 20, name="product_other"
    )
    (own,) = product(
        [direct], integrals, late, cores[1:], where_to[half:], [own], 10 << 20, name="product_own"
    )
    swapped = lax.ppermute(other, "owner", owner_perm(lambda y, z, c: (y, z, 1 - c)))
    total = own + swapped
    total = sum_to_first(total.reshape(SIDE, SIDE, *total.shape[1:]), 0)
    total = sum_to_first(total, 1)
    return total.swapaxes(0, 1).reshape(pairs, ab)


def solution(mesh):
    placed = (P("owner", None, None, None), P(None, "owner", "task", None), P())
    return jax.shard_map(
        per_device, mesh=mesh, in_specs=placed, out_specs=P("owner", "task"), check_vma=False
    )
```

```python
import functools

import jax
import jax.numpy as jnp
from jax import lax
from jax.experimental import pallas as pl
from jax.experimental.pallas import tpu as pltpu
from jax.sharding import PartitionSpec as P

OWNERS, TASKS, SIDE = 32, 4, 4
WHOLE, HALVES, LANES = 2, 2, 128
UNITS = WHOLE * HALVES + 1
SHARED = UNITS * TASKS // HALVES
BUNDLE = 5
GROUP = 8
F32 = jnp.float32


def owner_at(y, z, c):
    return ((y % SIDE) * SIDE + z % SIDE) * 2 + c


def owner_perm(move):
    return [
        (owner_at(y, z, c), owner_at(*move(y, z, c)))
        for y in range(SIDE)
        for z in range(SIDE)
        for c in range(2)
    ]


def along(step, cores_swapped):
    return owner_perm(
        lambda y, z, c: (y, z + step, c) if c == cores_swapped else (y + step, z, c)
    )


def shift_task(step):
    return [(t, (t + step) % TASKS) for t in range(TASKS)]


def pack_kernel(by_task, nz_ref, amp_ref, out_ref, listed, source, nz_sem, sem):
    owners, count, pairs, _ = out_ref.shape
    tiles, _, _, ct = source.shape
    task = lax.axis_index("task")
    copies = [pltpu.make_async_copy(nz_ref, listed, nz_sem)]
    for k in range(tiles):
        copies.append(pltpu.make_async_copy(amp_ref.at[:, k], source.at[k], sem.at[k]))
    for copy in copies:
        copy.start()

    n = pairs * GROUP
    row = lax.broadcasted_iota(jnp.int32, (n, n), 0)
    column = lax.broadcasted_iota(jnp.int32, (n, n), 1)
    turn = (row == column % GROUP * pairs + column // GROUP).astype(F32).astype(source.dtype)
    for copy in copies:
        copy.wait()

    def block(o, slot):
        j = o % GROUP
        rows = source[listed[slot, o], :, o - j : o - j + GROUP].reshape(n, ct)
        product = jnp.dot(turn[j * pairs : (j + 1) * pairs], rows, preferred_element_type=F32)
        return product.astype(out_ref.dtype)

    def give(i, carry):
        for o in range(owners):
            out_ref[o, i] = block(o, SHARED + i)
        return carry

    def give_units(i, carry):
        for o in range(owners):
            both = block(o, task * WHOLE + i)
            for h in range(HALVES):
                out_ref[o, HALVES * i + h] = both[:, h * LANES : (h + 1) * LANES]
        return carry

    if not by_task:
        lax.fori_loop(0, count, give, 0)
        return
    lax.fori_loop(0, WHOLE, give_units, 0)
    for o in range(owners):
        both = block(o, TASKS * WHOLE + task // HALVES)
        halves = [both[:, h * LANES : (h + 1) * LANES] for h in range(HALVES)]
        out_ref[o, UNITS - 1] = jnp.where(task % HALVES == 0, *halves)


def pack(amplitudes, listed, by_task):
    pairs, tiles, owners, ct = amplitudes.shape
    count, width = (UNITS, LANES) if by_task else (listed.shape[0] - SHARED, ct)
    anywhere = pl.BlockSpec(memory_space=pltpu.HBM)
    return pl.pallas_call(
        functools.partial(pack_kernel, by_task),
        in_specs=[anywhere, anywhere],
        out_specs=pl.BlockSpec(memory_space=pltpu.VMEM),
        out_shape=jax.ShapeDtypeStruct((owners, count, pairs, width), amplitudes.dtype),
        scratch_shapes=[
            pltpu.SMEM(listed.shape, jnp.int32),
            pltpu.VMEM((tiles, pairs, owners, ct), amplitudes.dtype),
            pltpu.SemaphoreType.DMA,
            pltpu.SemaphoreType.DMA((tiles,)),
        ],
        compiler_params=pltpu.CompilerParams(vmem_limit_bytes=60 << 20),
        cost_estimate=pl.CostEstimate(
            flops=2 * count * owners * pairs * pairs * GROUP * ct * 8,
            bytes_accessed=2 * tiles * owners * pairs * ct,
            transcendentals=0,
        ),
        name="pack_shared" if by_task else "pack_direct",
    )(listed, amplitudes)


def product_kernel(pieces, plan, sides, on_top, cuts, slots_ref, half_ref, core_ref, places_ref, *refs):
    refs = list(refs)

    def take(n):
        taken = refs[:n]
        del refs[:n]
        return taken

    piece_refs, (int_ref,) = take(pieces), take(1)
    start_refs, out_refs, parts = take(sides * on_top), take(sides * len(cuts)), take(sides)
    held, rhs, held_sem, rhs_sem, part_sem, out_sem = refs
    blocks, pairs, ab = parts[0].shape
    steps = rhs_sem.shape[0]
    tile = ab // steps
    slots = len(plan)

    def columns(n):
        return pl.ds(n * tile if isinstance(n, int) else pl.multiple_of(n * tile, tile), tile)

    def fetches(n, l):
        if l < slots - 1:
            yield pltpu.make_async_copy(
                int_ref.at[slots_ref[l], 0, columns(n)], rhs.at[l, columns(n)], rhs_sem.at[n, l]
            )
            return
        for h in range(HALVES):
            lanes = pl.ds(pl.multiple_of(half_ref[h] * LANES, LANES), LANES)
            yield pltpu.make_async_copy(
                int_ref.at[slots_ref[l + h], 0, columns(n), lanes],
                rhs.at[l, columns(n), h * LANES : (h + 1) * LANES],
                rhs_sem.at[n, l + h],
            )

    def rows(i, l):
        for m, (p, j, part, parts_in_all, h) in enumerate(plan[l]):
            share = blocks // parts_in_all
            to = held.at[l, pl.ds(i * blocks + part * share, share)]
            if h is not None:
                to = to.at[:, :, h * LANES : (h + 1) * LANES]
            yield pltpu.make_async_copy(piece_refs[p].at[:, core_ref[i], j], to, held_sem.at[i, l, m])

    def fetch_start(n, i):
        return pltpu.make_async_copy(
            start_refs[i].at[:, :, columns(n)], parts[i].at[:, :, columns(n)], part_sem.at[n, i]
        )

    def puts(n, i):
        first = 0
        for k, size in enumerate(cuts):
            yield pltpu.make_async_copy(
                parts[i].at[first : first + size, :, columns(n)],
                out_refs[i * len(cuts) + k].at[:, :, columns(n)],
                out_sem.at[n, i, k],
            )
            first += size

    def bring(n, group):
        for l in group:
            for copy in fetches(n, l):
                copy.start()
        if on_top and group[0] == 0:
            for i in range(sides):
                fetch_start(n, i).start()

    groups = [range(l, min(l + BUNDLE, slots)) for l in range(0, slots, BUNDLE)]

    def step(n, first):
        here = columns(n)
        total = None
        for group in groups:
            for l in group:
                if first:
                    for i in range(sides):
                        for copy in rows(i, l):
                            copy.wait()
                for copy in fetches(n, l):
                    copy.wait()

            @pl.when(n + 1 < steps)
            def _(group=group):
                bring(n + 1, group)

            for l in group:
                term = lax.dot_general(
                    held[l].reshape(sides * blocks * pairs, -1),
                    rhs[l, here],
                    (((1,), (1,)), ((), ())),
                    preferred_element_type=F32,
                )
                total = term if total is None else total + term
        total = total.reshape(sides, blocks, pairs, tile)
        for i in range(sides):
            sums = total[i]
            if on_top:
                fetch_start(n, i).wait()
            for b in range(blocks):
                place = places_ref[i * blocks + b]
                before = parts[i][place, :, here] if on_top else 0
                parts[i][place, :, here] = sums[b] + before
            for copy in puts(n, i):
                copy.start()

    for group in groups:
        for i in range(sides):
            for l in group:
                for copy in rows(i, l):
                    copy.start()
        bring(0, group)
    step(0, True)
    lax.fori_loop(1, steps, lambda n, carry: (step(n, False), carry)[1], 0)
    for n in range(steps):
        for i in range(sides):
            for copy in puts(n, i):
                copy.wait()


def product(pieces, plan, integrals, slots, half, cores, places, start=(), cuts=None, spare=0, tile=512, name="product"):
    ab, ct = integrals.shape[2:]
    blocks, pairs, sides, count = OWNERS // 2, pieces[0].shape[2], cores.shape[0], len(plan)
    pieces = [piece.reshape(piece.shape[0] // 2, 2, *piece.shape[1:]) for piece in pieces]
    small = pl.BlockSpec(memory_space=pltpu.SMEM)
    anywhere = pl.BlockSpec(memory_space=pl.ANY)
    steps, cuts = ab // tile, cuts or (blocks,)
    part = (blocks, pairs, ab)
    return pl.pallas_call(
        functools.partial(product_kernel, len(pieces), plan, sides, len(start) > 0, cuts),
        in_specs=[small] * 4 + [anywhere] * (len(pieces) + 1 + len(start)),
        out_specs=[anywhere] * (sides * len(cuts)),
        out_shape=[jax.ShapeDtypeStruct((size, *part[1:]), F32) for size in cuts] * sides,
        scratch_shapes=[pltpu.VMEM(part, F32)] * sides
        + [
            pltpu.VMEM((count, sides * blocks, pairs, ct), integrals.dtype),
            pltpu.VMEM((count, ab, ct), integrals.dtype),
            pltpu.SemaphoreType.DMA((sides, count, max(map(len, plan)))),
            pltpu.SemaphoreType.DMA((steps, count + 1)),
            pltpu.SemaphoreType.DMA((steps, sides)),
            pltpu.SemaphoreType.DMA((steps, sides, len(cuts))),
        ],
        compiler_params=pltpu.CompilerParams(vmem_limit_bytes=(60 - spare) << 20),
        cost_estimate=pl.CostEstimate(
            flops=2 * sides * blocks * pairs * ab * count * ct,
            bytes_accessed=ab * count * ct * 2 + sides * blocks * pairs * ab * 4,
            transcendentals=0,
        ),
        name=name,
    )(slots, half, cores, places, *pieces, integrals, *start)


def send(x, step, swapped=0):
    return lax.ppermute(x, "owner", along(step, swapped))


def trade(x):
    return lax.ppermute(x, "owner", owner_perm(lambda y, z, c: (y, z, 1 - c)))


def per_device(amplitudes, integrals, nonzero_tiles):
    owner = lax.axis_index("owner")
    task = lax.axis_index("task")
    y, z, c = owner // (2 * SIDE), owner // 2 % SIDE, owner % 2
    pairs = amplitudes.shape[0]
    ab = integrals.shape[2]
    mine = lax.dynamic_index_in_dim(nonzero_tiles, owner, 0, False)

    listed = nonzero_tiles.T
    live = listed.shape[0]
    shared = pack(amplitudes, listed, True)
    quarter = lax.all_to_all(shared, "owner", 0, 0, tiled=True)
    direct = pack(amplitudes, listed, False)
    direct = lax.all_to_all(direct, "owner", 0, 0, tiled=True)
    before = lax.ppermute(quarter, "task", shift_task(1))
    after = lax.ppermute(quarter, "task", shift_task(-1))
    across = [
        lax.ppermute(before[: OWNERS // 2], "task", shift_task(1)),
        lax.ppermute(after[OWNERS // 2 :], "task", shift_task(-1)),
    ]

    def whole_slots(t):
        return t % TASKS * WHOLE + jnp.arange(WHOLE)

    def half_slots(*tasks):
        tasks = jnp.stack(tasks) % TASKS
        return TASKS * WHOLE + tasks // HALVES, tasks % HALVES

    near_ids, near_half = half_slots(task, task - 1)
    late_ids, late_half = half_slots(task + 1, task + 2)
    near_slots = [whole_slots(task), whole_slots(task - 1), whole_slots(task + 1), near_ids]
    late_slots = [jnp.arange(SHARED, live), whole_slots(task + 2), late_ids]
    slots = jnp.take(mine, jnp.concatenate(near_slots + late_slots))
    cut = 3 * WHOLE + HALVES
    near_slots, late_slots = slots[:cut], slots[cut:]

    def units(sources, j):
        return [(p, HALVES * j + h, k, len(sources), h) for k, p in enumerate(sources) for h in range(HALVES)]

    last = UNITS - 1
    near_plan = [units([p], j) for p in range(3) for j in range(WHOLE)] + [[(0, last, 0, 1, 0), (1, last, 0, 1, 1)]]
    late_plan = [[(0, j, 0, 1, None)] for j in range(live - SHARED)] + [units([2, 3], j) for j in range(WHOLE)]
    late_plan.append([(1, last, 0, 1, 0), (2, last, 0, 2, 1), (3, last, 1, 2, 1)])

    def places(core):
        dy = (jnp.repeat(jnp.arange(SIDE), SIDE) - y) % SIDE
        dz = (jnp.tile(jnp.arange(SIDE), SIDE) - z) % SIDE
        first, second = jnp.where(core == 0, dz, dy), jnp.where(core == 0, dy, dz)
        return (first % 2 * 2 + first // 2) * SIDE + second

    cores = jnp.stack([1 - c, c])
    where_to = jnp.concatenate([places(1 - c), places(c)])
    both = product(
        [quarter, before, after], near_plan, integrals, near_slots, near_half, cores, where_to, spare=4, name="product_near"
    )
    parts = product(
        [direct, after, *across],
        late_plan,
        integrals,
        late_slots,
        late_half,
        cores,
        where_to,
        both,
        (SIDE, SIDE, 2 * SIDE),
        8,
        name="product_late",
    )
    theirs, ours = ([x.reshape(-1, SIDE, *x.shape[1:]) for x in parts[i : i + 3]] for i in (0, 3))
    farthest = (ours[1] + trade(theirs[1]))[0]
    theirs[0], theirs[2], farthest = lax.optimization_barrier((theirs[0], theirs[2], farthest))
    total = send(farthest, 2)
    sides = ours[2] + trade(theirs[2])
    staying = (ours[0] + trade(theirs[0]))[0]
    total = staying + total + send(sides[0], 1) + send(sides[1], 3)
    return total[0] + send(total[2], 2, 1) + send(total[1], 1, 1) + send(total[3], 3, 1)


def solution(mesh):
    placed = (P("owner", None, None, None), P(None, "owner", "task", None), P())
    return jax.shard_map(
        per_device, mesh=mesh, in_specs=placed, out_specs=P("owner", "task"), check_vma=False
    )
```

```python
import functools

import jax
import jax.numpy as jnp
from jax import lax
from jax.experimental import pallas as pl
from jax.experimental.pallas import tpu as pltpu
from jax.sharding import PartitionSpec as P

OWNERS, TASKS, SIDE = 32, 4, 4
WHOLE, HALVES, LANES = 2, 2, 128
UNITS = WHOLE * HALVES + 1
SHARED = UNITS * TASKS // HALVES
BUNDLE = 5
GROUP = 8
F32 = jnp.float32


def owner_at(y, z, c):
    return ((y % SIDE) * SIDE + z % SIDE) * 2 + c


def owner_perm(move):
    return [
        (owner_at(y, z, c), owner_at(*move(y, z, c)))
        for y in range(SIDE)
        for z in range(SIDE)
        for c in range(2)
    ]


def along(step, cores_swapped):
    return owner_perm(
        lambda y, z, c: (y, z + step, c) if c == cores_swapped else (y + step, z, c)
    )


def shift_task(step):
    return [(t, (t + step) % TASKS) for t in range(TASKS)]


def pack_kernel(by_task, nz_ref, amp_ref, out_ref, listed, source, nz_sem, sem):
    owners, count, pairs, _ = out_ref.shape
    tiles, _, _, ct = source.shape
    task = lax.axis_index("task")
    half = owners // 2

    def fetch(side, k):
        here = slice(side * half, (side + 1) * half)
        return pltpu.make_async_copy(amp_ref.at[:, k, here], source.at[k, :, here], sem.at[side, k])

    listing = pltpu.make_async_copy(nz_ref, listed, nz_sem)
    listing.start()
    for side in range(2):
        for k in range(tiles):
            fetch(side, k).start()

    n = pairs * GROUP
    row = lax.broadcasted_iota(jnp.int32, (n, n), 0)
    column = lax.broadcasted_iota(jnp.int32, (n, n), 1)
    turn = (row == column % GROUP * pairs + column // GROUP).astype(F32).astype(source.dtype)
    listing.wait()

    def block(o, slot):
        j = o % GROUP
        rows = source[listed[slot, o], :, o - j : o - j + GROUP].reshape(n, ct)
        product = jnp.dot(turn[j * pairs : (j + 1) * pairs], rows, preferred_element_type=F32)
        return product.astype(out_ref.dtype)

    for side in range(2):
        for k in range(tiles):
            fetch(side, k).wait()
        here = range(side * half, (side + 1) * half)

        def give(i, carry, here=here):
            for o in here:
                out_ref[o, i] = block(o, SHARED + i)
            return carry

        def give_units(i, carry, here=here):
            for o in here:
                both = block(o, task * WHOLE + i)
                for h in range(HALVES):
                    out_ref[o, HALVES * i + h] = both[:, h * LANES : (h + 1) * LANES]
            return carry

        if not by_task:
            lax.fori_loop(0, count, give, 0)
            continue
        lax.fori_loop(0, WHOLE, give_units, 0)
        for o in here:
            both = block(o, TASKS * WHOLE + task // HALVES)
            halves = [both[:, h * LANES : (h + 1) * LANES] for h in range(HALVES)]
            out_ref[o, UNITS - 1] = jnp.where(task % HALVES == 0, *halves)


def pack(amplitudes, listed, by_task):
    pairs, tiles, owners, ct = amplitudes.shape
    count, width = (UNITS, LANES) if by_task else (listed.shape[0] - SHARED, ct)
    anywhere = pl.BlockSpec(memory_space=pltpu.HBM)
    return pl.pallas_call(
        functools.partial(pack_kernel, by_task),
        in_specs=[anywhere, anywhere],
        out_specs=pl.BlockSpec(memory_space=pltpu.VMEM),
        out_shape=jax.ShapeDtypeStruct((owners, count, pairs, width), amplitudes.dtype),
        scratch_shapes=[
            pltpu.SMEM(listed.shape, jnp.int32),
            pltpu.VMEM((tiles, pairs, owners, ct), amplitudes.dtype),
            pltpu.SemaphoreType.DMA,
            pltpu.SemaphoreType.DMA((2, tiles)),
        ],
        compiler_params=pltpu.CompilerParams(vmem_limit_bytes=60 << 20),
        cost_estimate=pl.CostEstimate(
            flops=2 * count * owners * pairs * pairs * GROUP * ct * 8,
            bytes_accessed=2 * tiles * owners * pairs * ct,
            transcendentals=0,
        ),
        name="pack_shared" if by_task else "pack_direct",
    )(listed, amplitudes)


def product_kernel(pieces, plan, sides, on_top, cuts, slots_ref, half_ref, core_ref, places_ref, *refs):
    refs = list(refs)

    def take(n):
        taken = refs[:n]
        del refs[:n]
        return taken

    piece_refs, (int_ref,) = take(pieces), take(1)
    start_refs, out_refs, parts = take(sides * on_top), take(sides * len(cuts)), take(sides)
    held, rhs, held_sem, rhs_sem, part_sem, out_sem = refs
    blocks, pairs, ab = parts[0].shape
    steps = rhs_sem.shape[0]
    tile = ab // steps
    slots = len(plan)

    def columns(n):
        return pl.ds(n * tile if isinstance(n, int) else pl.multiple_of(n * tile, tile), tile)

    def fetches(n, l):
        if l < slots - 1:
            yield pltpu.make_async_copy(
                int_ref.at[slots_ref[l], 0, columns(n)], rhs.at[l, columns(n)], rhs_sem.at[n, l]
            )
            return
        for h in range(HALVES):
            lanes = pl.ds(pl.multiple_of(half_ref[h] * LANES, LANES), LANES)
            yield pltpu.make_async_copy(
                int_ref.at[slots_ref[l + h], 0, columns(n), lanes],
                rhs.at[l, columns(n), h * LANES : (h + 1) * LANES],
                rhs_sem.at[n, l + h],
            )

    def rows(i, l):
        for m, (p, j, part, parts_in_all, h) in enumerate(plan[l]):
            share = blocks // parts_in_all
            to = held.at[l, pl.ds(i * blocks + part * share, share)]
            if h is not None:
                to = to.at[:, :, h * LANES : (h + 1) * LANES]
            yield pltpu.make_async_copy(piece_refs[p].at[:, core_ref[i], j], to, held_sem.at[i, l, m])

    def fetch_start(n, i):
        return pltpu.make_async_copy(
            start_refs[i].at[:, :, columns(n)], parts[i].at[:, :, columns(n)], part_sem.at[n, i]
        )

    def puts(n, i):
        first = 0
        for k, size in enumerate(cuts):
            yield pltpu.make_async_copy(
                parts[i].at[first : first + size, :, columns(n)],
                out_refs[i * len(cuts) + k].at[:, :, columns(n)],
                out_sem.at[n, i, k],
            )
            first += size

    def bring(n, group):
        for l in group:
            for copy in fetches(n, l):
                copy.start()
        if on_top and group[0] == 0:
            for i in range(sides):
                fetch_start(n, i).start()

    groups = [range(l, min(l + BUNDLE, slots)) for l in range(0, slots, BUNDLE)]

    def step(n, first):
        here = columns(n)
        total = None
        for group in groups:
            for l in group:
                if first:
                    for i in range(sides):
                        for copy in rows(i, l):
                            copy.wait()
                for copy in fetches(n, l):
                    copy.wait()

            @pl.when(n + 1 < steps)
            def _(group=group):
                bring(n + 1, group)

            for l in group:
                term = lax.dot_general(
                    held[l].reshape(sides * blocks * pairs, -1),
                    rhs[l, here],
                    (((1,), (1,)), ((), ())),
                    preferred_element_type=F32,
                )
                total = term if total is None else total + term
        total = total.reshape(sides, blocks, pairs, tile)
        for i in range(sides):
            sums = total[i]
            if on_top:
                fetch_start(n, i).wait()
            for b in range(blocks):
                place = places_ref[i * blocks + b]
                before = parts[i][place, :, here] if on_top else 0
                parts[i][place, :, here] = sums[b] + before
            for copy in puts(n, i):
                copy.start()

    for group in groups:
        for i in range(sides):
            for l in group:
                for copy in rows(i, l):
                    copy.start()
        bring(0, group)
    step(0, True)
    lax.fori_loop(1, steps, lambda n, carry: (step(n, False), carry)[1], 0)
    for n in range(steps):
        for i in range(sides):
            for copy in puts(n, i):
                copy.wait()


def product(pieces, plan, integrals, slots, half, cores, places, start=(), cuts=None, spare=0, tile=512, name="product"):
    ab, ct = integrals.shape[2:]
    blocks, pairs, sides, count = OWNERS // 2, pieces[0].shape[2], cores.shape[0], len(plan)
    pieces = [piece.reshape(piece.shape[0] // 2, 2, *piece.shape[1:]) for piece in pieces]
    small = pl.BlockSpec(memory_space=pltpu.SMEM)
    anywhere = pl.BlockSpec(memory_space=pl.ANY)
    steps, cuts = ab // tile, cuts or (blocks,)
    part = (blocks, pairs, ab)
    return pl.pallas_call(
        functools.partial(product_kernel, len(pieces), plan, sides, len(start) > 0, cuts),
        in_specs=[small] * 4 + [anywhere] * (len(pieces) + 1 + len(start)),
        out_specs=[anywhere] * (sides * len(cuts)),
        out_shape=[jax.ShapeDtypeStruct((size, *part[1:]), F32) for size in cuts] * sides,
        scratch_shapes=[pltpu.VMEM(part, F32)] * sides
        + [
            pltpu.VMEM((count, sides * blocks, pairs, ct), integrals.dtype),
            pltpu.VMEM((count, ab, ct), integrals.dtype),
            pltpu.SemaphoreType.DMA((sides, count, max(map(len, plan)))),
            pltpu.SemaphoreType.DMA((steps, count + 1)),
            pltpu.SemaphoreType.DMA((steps, sides)),
            pltpu.SemaphoreType.DMA((steps, sides, len(cuts))),
        ],
        compiler_params=pltpu.CompilerParams(vmem_limit_bytes=(60 - spare) << 20),
        cost_estimate=pl.CostEstimate(
            flops=2 * sides * blocks * pairs * ab * count * ct,
            bytes_accessed=ab * count * ct * 2 + sides * blocks * pairs * ab * 4,
            transcendentals=0,
        ),
        name=name,
    )(slots, half, cores, places, *pieces, integrals, *start)


def send(x, step, swapped=0):
    return lax.ppermute(x, "owner", along(step, swapped))


def trade(x):
    return lax.ppermute(x, "owner", owner_perm(lambda y, z, c: (y, z, 1 - c)))


def per_device(amplitudes, integrals, nonzero_tiles):
    owner = lax.axis_index("owner")
    task = lax.axis_index("task")
    y, z, c = owner // (2 * SIDE), owner // 2 % SIDE, owner % 2
    pairs = amplitudes.shape[0]
    ab = integrals.shape[2]
    mine = lax.dynamic_index_in_dim(nonzero_tiles, owner, 0, False)

    listed = nonzero_tiles.T
    live = listed.shape[0]
    shared = pack(amplitudes, listed, True)
    quarter = lax.all_to_all(shared, "owner", 0, 0, tiled=True)
    direct = pack(amplitudes, listed, False)
    direct = lax.all_to_all(direct, "owner", 0, 0, tiled=True)
    before = lax.ppermute(quarter, "task", shift_task(1))
    after = lax.ppermute(quarter, "task", shift_task(-1))
    across = [
        lax.ppermute(before[: OWNERS // 2], "task", shift_task(1)),
        lax.ppermute(after[OWNERS // 2 :], "task", shift_task(-1)),
    ]

    def whole_slots(t):
        return t % TASKS * WHOLE + jnp.arange(WHOLE)

    def half_slots(*tasks):
        tasks = jnp.stack(tasks) % TASKS
        return TASKS * WHOLE + tasks // HALVES, tasks % HALVES

    near_ids, near_half = half_slots(task, task - 1)
    late_ids, late_half = half_slots(task + 1, task + 2)
    near_slots = [whole_slots(task), whole_slots(task - 1), whole_slots(task + 1), near_ids]
    late_slots = [jnp.arange(SHARED, live), whole_slots(task + 2), late_ids]
    slots = jnp.take(mine, jnp.concatenate(near_slots + late_slots))
    cut = 3 * WHOLE + HALVES
    near_slots, late_slots = slots[:cut], slots[cut:]

    def units(sources, j):
        return [(p, HALVES * j + h, k, len(sources), h) for k, p in enumerate(sources) for h in range(HALVES)]

    last = UNITS - 1
    near_plan = [units([p], j) for p in range(3) for j in range(WHOLE)] + [[(0, last, 0, 1, 0), (1, last, 0, 1, 1)]]
    late_plan = [[(0, j, 0, 1, None)] for j in range(live - SHARED)] + [units([2, 3], j) for j in range(WHOLE)]
    late_plan.append([(1, last, 0, 1, 0), (2, last, 0, 2, 1), (3, last, 1, 2, 1)])

    def places(core):
        dy = (jnp.repeat(jnp.arange(SIDE), SIDE) - y) % SIDE
        dz = (jnp.tile(jnp.arange(SIDE), SIDE) - z) % SIDE
        first, second = jnp.where(core == 0, dz, dy), jnp.where(core == 0, dy, dz)
        return (first % 2 * 2 + first // 2) * SIDE + second

    cores = jnp.stack([1 - c, c])
    where_to = jnp.concatenate([places(1 - c), places(c)])
    both = product(
        [quarter, before, after], near_plan, integrals, near_slots, near_half, cores, where_to, spare=5, name="product_near"
    )
    parts = product(
        [direct, after, *across],
        late_plan,
        integrals,
        late_slots,
        late_half,
        cores,
        where_to,
        both,
        (SIDE, SIDE, 2 * SIDE),
        14,
        name="product_late",
    )
    theirs, ours = ([x.reshape(-1, SIDE, *x.shape[1:]) for x in parts[i : i + 3]] for i in (0, 3))
    farthest = (ours[1] + trade(theirs[1]))[0]
    theirs[0], theirs[2], farthest = lax.optimization_barrier((theirs[0], theirs[2], farthest))
    total = send(farthest, 2)
    sides = ours[2] + trade(theirs[2])
    staying = (ours[0] + trade(theirs[0]))[0]
    total = staying + total + send(sides[0], 1) + send(sides[1], 3)
    return total[0] + send(total[2], 2, 1) + send(total[1], 1, 1) + send(total[3], 3, 1)


def solution(mesh):
    placed = (P("owner", None, None, None), P(None, "owner", "task", None), P())
    return jax.shard_map(
        per_device, mesh=mesh, in_specs=placed, out_specs=P("owner", "task"), check_vma=False
    )
```
